768 devices in a mesh: dp: 96 (over y, z_lo, x), tensor: 8 (over z_hi, core).
Axes of the slice: x: 4, y: 8, z: 12 (z_hi: 4, z_lo: 3; z = z_hi * 3 + z_lo), core: 2. Of those that a mesh axis runs over, the one named last changes fastest.
Arguments:
- inputs: bfloat16 [98304, 8192], P('dp', 'tensor'), may hold values from -6 to 6
- key_weight: bfloat16 [768, 8192], P('dp', 'tensor'), may hold values from -0.0625 to 0.0625
- key_cotangent: bfloat16 [98304, 768], P(('dp', 'tensor')), may hold values from -24 to 24
Outputs:
- key_out: bfloat16 [98304, 768], P(('dp', 'tensor'))
- input_grad: bfloat16 [98304, 8192], P('dp', 'tensor')
- weight_grad: float32 [768, 8192], P('dp', 'tensor')
The draws below stay inside these ranges and needn't reach their ends.
All inputs are finite; a program needn't handle non-finite values.
Results may differ from the reference program's by a relative error of at most 0.001.
Values may be sent and summed in bfloat16 or wider, within the bound.
A program may use at most 32 MiB of HBM per device.

```python
import jax
import jax.numpy as jnp
from jax import lax

D = 8192
HEAD_DIM = 128
KV_HEADS = 6
TOK_DEV = 128
KCOLS = 768
TOKENS = 98304
N_DP = 96
N_TENSOR = 8


def raised(values, rng, source, target, shards_of, factor):
    def block_of(position):
        return (jnp.arange(values.shape[position]) // (values.shape[position] // shards_of)).reshape((-1,) + (1,) * (values.ndim - 1 - position))

    near = jax.random.permutation(rng, shards_of)[block_of(target)]
    second = (block_of(target) + shards_of // 2) % shards_of
    return jnp.where((block_of(source) == near) | (block_of(source) == second), factor * values, values)


def block_levels(rng, shape, shards, low, high):
    factor_of, own = 1.0, jax.random.fold_in(rng, 6)
    for axis_at, parts in shards:
        heights = jnp.exp(jax.random.uniform(jax.random.fold_in(own, axis_at), (parts,), jnp.float32, low / len(shards), high / len(shards)))
        factor_of = factor_of * jnp.repeat(heights, shape[axis_at] // parts).reshape([-1 if axis == axis_at else 1 for axis in range(len(shape))])
    return factor_of


def scatter_about(key, dims, deviation, limit, cuts=(), held_as=jnp.bfloat16):
    drawn = deviation * jax.random.normal(key, dims, jnp.float32)
    if cuts:
        drawn = drawn * block_levels(key, dims, cuts, -0.22, 0.18)
    return jnp.clip(drawn, -limit, limit).astype(held_as)


def heavy_noise(rng, extent, scale, reach, shards, heavy, kind=jnp.bfloat16):
    array = scale * jax.random.normal(rng, extent, jnp.float32)
    if shards:
        array = array * block_levels(rng, extent, shards, -0.22, 0.18)
    return jnp.clip(raised(array, jax.random.fold_in(rng, 3), *heavy), -reach, reach).astype(kind)


def setup_inputs(seed: int = 0) -> dict:
    arg_keys = jax.random.split(jax.random.key(seed), 4)
    inputs = scatter_about(arg_keys[0], (TOKENS, D), 1.0, 6.0, ((0, 96), (1, 8)))
    key_weight = scatter_about(arg_keys[1], (KCOLS, D), D ** -0.5, 0.0625, ((0, 96), (1, 8)))
    key_cotangent = heavy_noise(arg_keys[2], (TOKENS, KCOLS), 1.0, 24.0, ((0, 768),), (0, 1, 768, 6.0))
    return {"inputs": inputs, "key_weight": key_weight, "key_cotangent": key_cotangent}


def reference(inputs, key_weight, key_cotangent):
    group_rows = TOK_DEV * N_TENSOR
    input_blocks = inputs.reshape(N_DP, group_rows, D)
    cot_blocks = key_cotangent.reshape(N_DP, group_rows, KV_HEADS * HEAD_DIM)

    def one_group(total, pair):
        row_block, cot_block = pair
        key_block = jnp.dot(row_block, key_weight.T, preferred_element_type=jnp.float32).astype(jnp.bfloat16)
        grad_block = jnp.dot(cot_block, key_weight, preferred_element_type=jnp.float32).astype(jnp.bfloat16)
        total = total + jnp.dot(cot_block.T, row_block, preferred_element_type=jnp.float32)
        return total, (key_block, grad_block)

    start_total = jnp.zeros((KV_HEADS * HEAD_DIM, D), jnp.float32)
    weight_grad, (key_out, input_grad) = lax.scan(one_group, start_total, (input_blocks, cot_blocks))
    return key_out.reshape(TOKENS, KV_HEADS * HEAD_DIM), input_grad.reshape(TOKENS, D), weight_grad
```

```python
import jax
import jax.numpy as jnp
from jax import lax
from jax.experimental import pallas as pl
from jax.experimental.pallas import tpu as pltpu
from jax.sharding import PartitionSpec as P

NX, NY, NL, NH = 4, 8, 3, 4
SUBS_W = 1
SUBS_G = 3
N_COPIES = 160
F32 = jnp.float32
BF16 = jnp.bfloat16


def kernel(
    x_hbm, w_ref, c_hbm,
    key_ref, grad_hbm, wg_ref,
    x_v, wx, wall, cot, part, part_in, key_a, key_b, g, g_half, g_in, gx_in, gz_in, grad_v,
    send_sems, recv_sems, local_sems,
):
    dp = lax.axis_index("dp")
    tn = lax.axis_index("tensor")
    x = dp % NX
    zl = (dp // NX) % NL
    y = dp // (NX * NL)
    core = tn % 2
    zh = tn // 2

    def at(x=x, zl=zl, y=y, zh=zh, core=core):
        return ((y * NL + zl) * NX + x, zh * 2 + core)

    y_up, y_down = (y + 1) % NY, (y + NY - 1) % NY
    h_up, h_down, h_far = (zh + 1) % NH, (zh + NH - 1) % NH, (zh + 2) % NH
    to_yup, to_ydown = at(y=y_up), at(y=y_down)
    to_hup, to_hdown = at(zh=h_up), at(zh=h_down)
    sibling = at(core=1 - core)

    used = [0]
    sends = []

    def send(src, dst, where):
        n = used[0]
        used[0] += 1
        copy = pltpu.make_async_remote_copy(
            src_ref=src, dst_ref=dst, send_sem=send_sems.at[n], recv_sem=recv_sems.at[n],
            device_id=where, device_id_type=pl.DeviceIdType.MESH,
        )
        copy.start()
        sends.append(copy)
        return copy

    load_x = pltpu.make_async_copy(x_hbm, x_v, local_sems.at[0])
    load_x.start()
    load_c = pltpu.make_async_copy(c_hbm, cot.at[tn], local_sems.at[1])
    load_c.start()
    wx[x] = w_ref[...].astype(F32)

    barrier = pltpu.get_barrier_semaphore()
    partners = [at(x=(x + d) % NX) for d in range(1, NX)]
    partners += [at(zl=(zl + d) % NL) for d in range(1, NL)]
    partners += [to_yup, to_ydown, to_hup, to_hdown, sibling]
    for partner in partners:
        pl.semaphore_signal(barrier, inc=1, device_id=partner, device_id_type=pl.DeviceIdType.MESH)
    pl.semaphore_wait(barrier, len(partners))

    w_x = [send(wx.at[x], wx.at[x], at(x=(x + d) % NX)) for d in range(1, NX)]
    load_c.wait()
    c_up = send(cot.at[tn], cot.at[tn], to_hup)
    c_down = send(cot.at[tn], cot.at[tn], to_hdown)
    c_sib = [send(cot.at[tn], cot.at[tn], sibling)]

    for copy in w_x:
        copy.wait_recv()
    mine = y * NL + zl
    wall[mine] = wx[...].reshape(32, 1024).astype(BF16)
    w_z = [send(wall.at[mine], wall.at[mine], at(zl=(zl + d) % NL)) for d in range(1, NL)]
    for copy in w_z:
        copy.wait_recv()

    def w_step(k, q):
        size = NL // SUBS_W
        up = ((y + NY - k) % NY) * NL + q * size
        down = ((y + k) % NY) * NL + q * size
        rows_up, rows_down = (pl.ds(0, 32), pl.ds(0, 32)) if k < 3 else (pl.ds(0, 16), pl.ds(16, 16))
        a = wall.at[pl.ds(up, size), rows_up]
        b = wall.at[pl.ds(down, size), rows_down]
        return send(a, a, to_yup), send(b, b, to_ydown)

    def w_ring(k, before):
        new = []
        for q in range(SUBS_W):
            if before:
                before[q][0].wait_recv()
                before[q][1].wait_recv()
            new.append(w_step(k, q))
        return new

    ring = w_ring(0, None)
    ring = w_ring(1, ring)
    ring = w_ring(2, ring)

    c_up.wait_recv()
    from_down = cot.at[h_down * 2 + core]
    c_far0 = send(from_down.at[pl.ds(0, 64)], from_down.at[pl.ds(0, 64)], to_hup)
    c_down.wait_recv()
    from_up = cot.at[h_up * 2 + core]
    c_far1 = send(from_up.at[pl.ds(64, 64)], from_up.at[pl.ds(64, 64)], to_hdown)
    c_sib.append(send(from_down, from_down, sibling))
    c_sib.append(send(from_up, from_up, sibling))

    ring = w_ring(3, ring)
    load_x.wait()
    for a, b in ring:
        a.wait_recv()
        b.wait_recv()

    s_part = []
    for j, h in enumerate((h_far, h_up, h_down, zh)):
        rows = pl.ds(pl.multiple_of(h * 256, 256), 256)
        prod = lax.dot_general(
            x_v[rows, :], wall[...].reshape(768, 1024), (((1,), (1,)), ((), ())), preferred_element_type=F32
        )
        part[j] = prod.reshape(2, 128, 768)
        s_part.append(send(part.at[j, 1 - core], part_in.at[j], sibling))

    def join(j):
        s_part[j].wait_recv()
        part[j, core] = part[j, core] + part_in[j]

    lo, hi = pl.ds(0, 64), pl.ds(64, 64)
    join(0)
    k_a0 = send(part.at[0, core, lo], key_a.at[0], to_hup)
    k_a1 = send(part.at[0, core, hi], key_a.at[1], to_hdown)
    join(1)
    k_b = [send(part.at[1, core, hi], key_b.at[0, hi], to_hup)]
    join(2)
    k_b.append(send(part.at[2, core, lo], key_b.at[1, lo], to_hdown))

    c_far0.wait_recv()
    c_far1.wait_recv()
    far = cot.at[h_far * 2 + core]
    c_sib.append(send(far, far, sibling))
    join(3)
    for copy in c_sib:
        copy.wait_recv()

    for q in range(3):
        left = cot[:, :, 256 * q : 256 * q + 256].reshape(1024, 256)
        prod = lax.dot_general(left, x_v[...], (((0,), (0,)), ((), ())), preferred_element_type=F32)
        g[8 * q : 8 * q + 8] = prod.reshape(8, 32, 1024)

    size = NL // SUBS_G

    def g_first(q):
        far_y = ((y + 4) % NY) * NL + q * size
        at_q = pl.ds(q * size, size)
        a = send(g.at[pl.ds(far_y, size), pl.ds(0, 16)], g_half.at[0, at_q], to_yup)
        b = send(g.at[pl.ds(far_y, size), pl.ds(16, 16)], g_half.at[1, at_q], to_ydown)
        return a, b

    def g_step(k, q, before):
        at_q = pl.ds(q * size, size)
        up = ((y + 4 - k) % NY) * NL + q * size
        down = ((y + 4 + k) % NY) * NL + q * size
        new = []
        for side, block, where in ((0, up, to_yup), (1, down, to_ydown)):
            before[side].wait_recv()
            here = pl.ds(block, size)
            if k == 1:
                rows = pl.ds(16 * side, 16)
                g[here, rows] = g[here, rows] + g_half[side, at_q]
            else:
                g[here] = g[here] + g_in[side, k - 2, at_q]
            new.append(send(g.at[here], g_in.at[side, k - 1, at_q], where))
        return new

    flow = [g_first(q) for q in range(SUBS_G)]

    def grad_chunk(i):
        prod = jnp.dot(
            cot[2 * i : 2 * i + 2].reshape(256, 768), wall[...].reshape(768, 1024), preferred_element_type=F32
        )
        grad_v[256 * i : 256 * i + 256] = prod.astype(BF16)

    grad_chunk(0)
    grad_chunk(1)
    for q in range(SUBS_G):
        flow[q] = g_step(1, q, flow[q])
    grad_chunk(2)
    grad_chunk(3)
    store_grad = pltpu.make_async_copy(grad_v, grad_hbm, local_sems.at[2])
    store_grad.start()

    k_a0.wait_recv()
    part[1, core, lo] = part[1, core, lo] + key_a[0]
    k_b.append(send(part.at[1, core, lo], key_b.at[0, lo], to_hup))
    k_a1.wait_recv()
    part[2, core, hi] = part[2, core, hi] + key_a[1]
    k_b.append(send(part.at[2, core, hi], key_b.at[1, hi], to_hdown))

    for k in (2, 3):
        for q in range(SUBS_G):
            flow[q] = g_step(k, q, flow[q])
    for q in range(SUBS_G):
        flow[q][0].wait_recv()
        flow[q][1].wait_recv()
    own = pl.ds(y * NL, NL)
    g[own] = g[own] + (g_in[0, 2] + g_in[1, 2])

    g_x = []
    for d in range(1, NX):
        to = (x + d) % NX
        g_x.append(send(g.at[own, pl.ds(pl.multiple_of(to * 8, 8), 8)], gx_in.at[x], at(x=to)))
    gx_in[x] = g[own, pl.ds(pl.multiple_of(x * 8, 8), 8)]
    for copy in g_x:
        copy.wait_recv()
    gz_in[3] = gx_in[0, 0] + gx_in[1, 0] + gx_in[2, 0] + gx_in[3, 0]
    gz_in[4] = gx_in[0, 1] + gx_in[1, 1] + gx_in[2, 1] + gx_in[3, 1]
    gz_in[5] = gx_in[0, 2] + gx_in[1, 2] + gx_in[2, 2] + gx_in[3, 2]
    g_z = []
    for d in range(1, NL):
        to = (zl + d) % NL
        g_z.append(send(gz_in.at[3 + to], gz_in.at[d], at(zl=to)))
    for copy in g_z:
        copy.wait_recv()
    wg_ref[...] = gz_in[3 + zl] + gz_in[1] + gz_in[2]

    for copy in k_b:
        copy.wait_recv()
    key_ref[...] = (part[3, core] + (key_b[0] + key_b[1])).astype(BF16)

    for copy in sends:
        copy.wait_send()
    store_grad.wait()


def body(inputs, key_weight, key_cotangent):
    vmem = pl.BlockSpec(memory_space=pltpu.VMEM)
    hbm = pl.BlockSpec(memory_space=pl.ANY)
    return pl.pallas_call(
        kernel,
        out_shape=(
            jax.ShapeDtypeStruct((128, 768), BF16),
            jax.ShapeDtypeStruct((1024, 1024), BF16),
            jax.ShapeDtypeStruct((8, 1024), F32),
        ),
        in_specs=[hbm, vmem, hbm],
        out_specs=(vmem, hbm, vmem),
        scratch_shapes=[
            pltpu.VMEM((1024, 1024), BF16),
            pltpu.VMEM((NX, 8, 1024), F32),
            pltpu.VMEM((24, 32, 1024), BF16),
            pltpu.VMEM((8, 128, 768), BF16),
            pltpu.VMEM((4, 2, 128, 768), F32),
            pltpu.VMEM((4, 128, 768), F32),
            pltpu.VMEM((2, 64, 768), F32),
            pltpu.VMEM((2, 128, 768), F32),
            pltpu.VMEM((24, 32, 1024), F32),
            pltpu.VMEM((2, 3, 16, 1024), F32),
            pltpu.VMEM((2, 3, 3, 32, 1024), F32),
            pltpu.VMEM((NX, NL, 8, 1024), F32),
            pltpu.VMEM((6, 8, 1024), F32),
            pltpu.VMEM((1024, 1024), BF16),
            pltpu.SemaphoreType.DMA((N_COPIES,)),
            pltpu.SemaphoreType.DMA((N_COPIES,)),
            pltpu.SemaphoreType.DMA((3,)),
        ],
        compiler_params=pltpu.CompilerParams(
            collective_id=0, has_side_effects=True, vmem_limit_bytes=48 * 1024 * 1024
        ),
        cost_estimate=pl.CostEstimate(flops=4_831_838_208, bytes_accessed=5_000_000, transcendentals=0),
    )(inputs, key_weight, key_cotangent)


def solution(mesh):
    in_specs = (P("dp", "tensor"), P("dp", "tensor"), P(("dp", "tensor"), None))
    out_specs = (P(("dp", "tensor"), None), P("dp", "tensor"), P("dp", "tensor"))
    return jax.shard_map(body, mesh=mesh, in_specs=in_specs, out_specs=out_specs, check_vma=False)
```

```python
import jax
import jax.numpy as jnp
from jax import lax
from jax.experimental import pallas as pl
from jax.experimental.pallas import tpu as pltpu
from jax.sharding import PartitionSpec as P

NX, NY, NL, NH = 4, 8, 3, 4
SUBS_W = 3
SUBS_G = 3
N_COPIES = 128
VMEM_MIB = 60
F32 = jnp.float32
BF16 = jnp.bfloat16


def kernel(
    x_hbm, w_ref, c_hbm,
    key_ref, grad_hbm, wg_ref,
    x_v, wx, wall, wabs, cot, part, part_in, key_a, key_b, g, a_half, a_in, ax_in, bx_a, bx_in, b_sum, b_half, b_in, gz, grad_v,
    send_sems, recv_sems, local_sems,
):
    dp = lax.axis_index("dp")
    tn = lax.axis_index("tensor")
    x = dp % NX
    zl = (dp // NX) % NL
    y = dp // (NX * NL)
    core = tn % 2
    zh = tn // 2

    def at(x=x, zl=zl, y=y, zh=zh, core=core):
        return ((y * NL + zl) * NX + x, zh * 2 + core)

    y_up, y_down = (y + 1) % NY, (y + NY - 1) % NY
    h_up, h_down, h_far = (zh + 1) % NH, (zh + NH - 1) % NH, (zh + 2) % NH
    to_yup, to_ydown = at(y=y_up), at(y=y_down)
    to_hup, to_hdown = at(zh=h_up), at(zh=h_down)
    sibling = at(core=1 - core)

    used = [0]
    sends = []

    def send(src, dst, where):
        n = used[0]
        used[0] += 1
        copy = pltpu.make_async_remote_copy(
            src_ref=src, dst_ref=dst, send_sem=send_sems.at[n], recv_sem=recv_sems.at[n],
            device_id=where, device_id_type=pl.DeviceIdType.MESH,
        )
        copy.start()
        sends.append(copy)
        return copy

    load_x = pltpu.make_async_copy(x_hbm, x_v, local_sems.at[0])
    load_x.start()
    load_c = pltpu.make_async_copy(c_hbm, cot.at[tn], local_sems.at[1])
    load_c.start()
    wx[x] = w_ref[...].astype(F32)

    barrier = pltpu.get_barrier_semaphore()
    partners = [at(x=(x + d) % NX) for d in range(1, NX)]
    partners += [at(zl=(zl + d) % NL) for d in range(1, NL)]
    partners += [to_yup, to_ydown, to_hup, to_hdown, sibling]
    for partner in partners:
        pl.semaphore_signal(barrier, inc=1, device_id=partner, device_id_type=pl.DeviceIdType.MESH)
    pl.semaphore_wait(barrier, len(partners))

    w_x = [send(wx.at[x], wx.at[x], at(x=(x + d) % NX)) for d in range(1, NX)]
    load_c.wait()
    c_up = send(cot.at[tn], cot.at[tn], to_hup)
    c_down = send(cot.at[tn], cot.at[tn], to_hdown)
    c_sib = [send(cot.at[tn], cot.at[tn], sibling)]

    for copy in w_x:
        copy.wait_recv()
    mine = NL + zl
    wall[mine] = wx[...].reshape(32, 1024).astype(BF16)
    w_z = [send(wall.at[mine], wall.at[mine], at(zl=(zl + d) % NL)) for d in range(1, NL)]
    for copy in w_z:
        copy.wait_recv()

    def w_step(k, q):
        size = NL // SUBS_W
        up, down = (1 - k) % NY, (1 + k) % NY
        rows_up, rows_down = (pl.ds(0, 32), pl.ds(0, 32)) if k < 3 else (pl.ds(0, 16), pl.ds(16, 16))

        def block(place, rows):
            return wall.at[pl.ds(place * NL + q * size, size), rows]

        return (
            send(block(up, rows_up), block((up - 1) % NY, rows_up), to_yup),
            send(block(down, rows_down), block((down + 1) % NY, rows_down), to_ydown),
        )

    def w_ring(k, before):
        new = []
        for q in range(SUBS_W):
            if before:
                before[q][0].wait_recv()
                before[q][1].wait_recv()
            new.append(w_step(k, q))
        return new

    lo, hi = pl.ds(0, 64), pl.ds(64, 64)
    ring = w_ring(0, None)
    ring = w_ring(1, ring)
    ring = w_ring(2, ring)

    c_up.wait_recv()
    from_down = cot.at[h_down * 2 + core]
    c_far0 = send(from_down.at[lo], from_down.at[lo], to_hup)
    c_down.wait_recv()
    from_up = cot.at[h_up * 2 + core]
    c_far1 = send(from_up.at[hi], from_up.at[hi], to_hdown)
    c_sib.append(send(from_down, from_down, sibling))
    c_sib.append(send(from_up, from_up, sibling))

    def key_product(n):
        out = []
        for j, h in enumerate((h_far, h_up, h_down, zh)):
            rows = pl.ds(pl.multiple_of(h * 256, 256), 256)
            prod = lax.dot_general(
                x_v[rows, :], wall[12 * n : 12 * n + 12].reshape(384, 1024), (((1,), (1,)), ((), ())),
                preferred_element_type=F32,
            )
            part[n, j] = prod.reshape(2, 128, 384)
            out.append(send(part.at[n, j, 1 - core], part_in.at[n, j], sibling))
        return out

    def key_first(n, halves):
        def join(j):
            halves[j].wait_recv()
            part[n, j, core] = part[n, j, core] + part_in[n, j]

        join(0)
        a0 = send(part.at[n, 0, core, lo], key_a.at[n, 0], to_hup)
        a1 = send(part.at[n, 0, core, hi], key_a.at[n, 1], to_hdown)
        join(1)
        b = [send(part.at[n, 1, core, hi], key_b.at[n, 0, hi], to_hup)]
        join(2)
        b.append(send(part.at[n, 2, core, lo], key_b.at[n, 1, lo], to_hdown))
        join(3)
        return a0, a1, b

    def key_relay(n, flows):
        a0, a1, b = flows
        a0.wait_recv()
        part[n, 1, core, lo] = part[n, 1, core, lo] + key_a[n, 0]
        b.append(send(part.at[n, 1, core, lo], key_b.at[n, 0, lo], to_hup))
        a1.wait_recv()
        part[n, 2, core, hi] = part[n, 2, core, hi] + key_a[n, 1]
        b.append(send(part.at[n, 2, core, hi], key_b.at[n, 1, hi], to_hdown))
        return b

    load_x.wait()
    halves = key_product(0)
    ring = w_ring(3, ring)
    flows0 = key_first(0, halves)

    for a, b in ring:
        a.wait_recv()
        b.wait_recv()
    halves = key_product(1)

    c_far0.wait_recv()
    c_far1.wait_recv()
    far = cot.at[h_far * 2 + core]
    c_sib.append(send(far, far, sibling))
    flows1 = key_first(1, halves)
    for copy in c_sib:
        copy.wait_recv()

    for q in range(3):
        left = cot[:, :, 256 * q : 256 * q + 256].reshape(1024, 256)
        prod = lax.dot_general(left, x_v[...], (((0,), (0,)), ((), ())), preferred_element_type=F32)
        g[8 * q : 8 * q + 8] = prod.reshape(8, 32, 1024)

    fa, fb = pl.ds(0, 512), pl.ds(512, 512)
    size = NL // SUBS_G

    def a_first(q):
        far_y = ((y + 4) % NY) * NL + q * size
        at_q = pl.ds(q * size, size)
        a = send(g.at[pl.ds(far_y, size), pl.ds(0, 16), fa], a_half.at[0, at_q], to_yup)
        b = send(g.at[pl.ds(far_y, size), pl.ds(16, 16), fa], a_half.at[1, at_q], to_ydown)
        return a, b

    def a_step(k, q, before):
        at_q = pl.ds(q * size, size)
        up = ((y + 4 - k) % NY) * NL + q * size
        down = ((y + 4 + k) % NY) * NL + q * size
        new = []
        for side, block, where in ((0, up, to_yup), (1, down, to_ydown)):
            before[side].wait_recv()
            here = pl.ds(block, size)
            if k == 1:
                rows = pl.ds(16 * side, 16)
                g[here, rows, fa] = g[here, rows, fa] + a_half[side, at_q]
            else:
                g[here, :, fa] = g[here, :, fa] + a_in[side, k - 2, at_q]
            new.append(send(g.at[here, :, fa], a_in.at[side, k - 1, at_q], where))
        return new

    x_up, x_down, x_far = (x + 1) % NX, (x + NX - 1) % NX, (x + 2) % NX
    to_xup, to_xdown = at(x=x_up), at(x=x_down)
    first, last = pl.ds(0, 12), pl.ds(12, 12)

    def rows_of(to):
        return pl.ds(pl.multiple_of(to * 8, 8), 8)

    a_flow = [a_first(q) for q in range(SUBS_G)]
    b_far0 = send(g.at[first, rows_of(x_far), fb], bx_a.at[0], to_xup)
    b_far1 = send(g.at[last, rows_of(x_far), fb], bx_a.at[1], to_xdown)
    b_x = [
        send(g.at[last, rows_of(x_up), fb], bx_in.at[0, last], to_xup),
        send(g.at[first, rows_of(x_down), fb], bx_in.at[1, first], to_xdown),
    ]

    for place in range(NY):
        wabs[pl.ds(((y + NY - 1 + place) % NY) * NL, NL)] = wall[NL * place : NL * place + NL]

    def grad_chunk(i):
        prod = jnp.dot(
            cot[2 * i : 2 * i + 2].reshape(256, 768), wabs[...].reshape(768, 1024), preferred_element_type=F32
        )
        grad_v[256 * i : 256 * i + 256] = prod.astype(BF16)

    grad_chunk(0)
    grad_chunk(1)
    for q in range(SUBS_G):
        a_flow[q] = a_step(1, q, a_flow[q])
    b_far0.wait_recv()
    g[first, rows_of(x_up), fb] = g[first, rows_of(x_up), fb] + bx_a[0]
    b_x.append(send(g.at[first, rows_of(x_up), fb], bx_in.at[0, first], to_xup))
    b_far1.wait_recv()
    g[last, rows_of(x_down), fb] = g[last, rows_of(x_down), fb] + bx_a[1]
    b_x.append(send(g.at[last, rows_of(x_down), fb], bx_in.at[1, last], to_xdown))
    k_b0 = key_relay(0, flows0)
    grad_chunk(2)
    grad_chunk(3)
    store_grad = pltpu.make_async_copy(grad_v, grad_hbm, local_sems.at[2])
    store_grad.start()
    for q in range(SUBS_G):
        a_flow[q] = a_step(2, q, a_flow[q])
    k_b1 = key_relay(1, flows1)

    for copy in b_x:
        copy.wait_recv()
    b_sum[...] = g[:, rows_of(x), fb] + (bx_in[0] + bx_in[1])

    def b_step(k, before):
        new = []
        for side, place, where in ((0, y + 4 - k, to_yup), (1, y + 4 + k, to_ydown)):
            here = pl.ds((place % NY) * NL, NL)
            lanes = pl.ds(256 * side, 256)
            if k > 0:
                before[side].wait_recv()
            if k == 0:
                new.append(send(b_sum.at[here, :, lanes], b_half.at[side], where))
                continue
            if k == 1:
                b_sum[here, :, lanes] = b_sum[here, :, lanes] + b_half[side]
            else:
                b_sum[here] = b_sum[here] + b_in[side, k - 2]
            new.append(send(b_sum.at[here], b_in.at[side, k - 1], where))
        return new

    b_flow = b_step(0, None)
    for q in range(SUBS_G):
        a_flow[q] = a_step(3, q, a_flow[q])
    for k in (1, 2, 3):
        b_flow = b_step(k, b_flow)
    for q in range(SUBS_G):
        a_flow[q][0].wait_recv()
        a_flow[q][1].wait_recv()
    own = pl.ds(y * NL, NL)
    g[own, :, fa] = g[own, :, fa] + (a_in[0, 2] + a_in[1, 2])
    a_x = []
    for d in range(1, NX):
        to = (x + d) % NX
        a_x.append(send(g.at[own, rows_of(to), fa], ax_in.at[x], at(x=to)))
    ax_in[x] = g[own, rows_of(x), fa]
    for copy in b_flow:
        copy.wait_recv()
    gz[pl.ds(3, 3), :, fb] = b_sum[own] + (b_in[0, 2] + b_in[1, 2])
    for copy in a_x:
        copy.wait_recv()
    gz[pl.ds(3, 3), :, fa] = (ax_in[0] + ax_in[1]) + (ax_in[2] + ax_in[3])

    g_z = []
    for d in range(1, NL):
        to = (zl + d) % NL
        g_z.append(send(gz.at[3 + to], gz.at[d], at(zl=to)))

    turn = ((y + NY - 1) % NY) * 96
    gap = lax.broadcasted_iota(jnp.int32, (768, 768), 1) - lax.broadcasted_iota(jnp.int32, (768, 768), 0)
    back = jnp.where((gap == turn) | (gap == turn - 768), 1.0, 0.0).astype(BF16)
    keys = None
    for n, copies in ((0, k_b0), (1, k_b1)):
        for copy in copies:
            copy.wait_recv()
        rel = (part[n, 3, core] + (key_b[n, 0] + key_b[n, 1])).astype(BF16)
        term = jnp.dot(rel, back[384 * n : 384 * n + 384], preferred_element_type=F32)
        keys = term if keys is None else keys + term
    key_ref[...] = keys.astype(BF16)

    for copy in g_z:
        copy.wait_recv()
    wg_ref[...] = gz[3 + zl] + gz[1] + gz[2]

    for copy in sends:
        copy.wait_send()
    store_grad.wait()


def body(inputs, key_weight, key_cotangent):
    vmem = pl.BlockSpec(memory_space=pltpu.VMEM)
    hbm = pl.BlockSpec(memory_space=pl.ANY)
    return pl.pallas_call(
        kernel,
        out_shape=(
            jax.ShapeDtypeStruct((128, 768), BF16),
            jax.ShapeDtypeStruct((1024, 1024), BF16),
            jax.ShapeDtypeStruct((8, 1024), F32),
        ),
        in_specs=[hbm, vmem, hbm],
        out_specs=(vmem, hbm, vmem),
        scratch_shapes=[
            pltpu.VMEM((1024, 1024), BF16),
            pltpu.VMEM((NX, 8, 1024), F32),
            pltpu.VMEM((24, 32, 1024), BF16),
            pltpu.VMEM((24, 32, 1024), BF16),
            pltpu.VMEM((8, 128, 768), BF16),
            pltpu.VMEM((2, 4, 2, 128, 384), F32),
            pltpu.VMEM((2, 4, 128, 384), F32),
            pltpu.VMEM((2, 2, 64, 384), F32),
            pltpu.VMEM((2, 2, 128, 384), F32),
            pltpu.VMEM((24, 32, 1024), F32),
            pltpu.VMEM((2, 3, 16, 512), F32),
            pltpu.VMEM((2, 3, 3, 32, 512), F32),
            pltpu.VMEM((NX, NL, 8, 512), F32),
            pltpu.VMEM((2, 12, 8, 512), F32),
            pltpu.VMEM((2, 24, 8, 512), F32),
            pltpu.VMEM((24, 8, 512), F32),
            pltpu.VMEM((2, 3, 8, 256), F32),
            pltpu.VMEM((2, 3, 3, 8, 512), F32),
            pltpu.VMEM((6, 8, 1024), F32),
            pltpu.VMEM((1024, 1024), BF16),
            pltpu.SemaphoreType.DMA((N_COPIES,)),
            pltpu.SemaphoreType.DMA((N_COPIES,)),
            pltpu.SemaphoreType.DMA((3,)),
        ],
        compiler_params=pltpu.CompilerParams(
            collective_id=0, has_side_effects=True, vmem_limit_bytes=VMEM_MIB * 1024 * 1024
        ),
        cost_estimate=pl.CostEstimate(flops=4_831_838_208, bytes_accessed=5_000_000, transcendentals=0),
    )(inputs, key_weight, key_cotangent)


def solution(mesh):
    in_specs = (P("dp", "tensor"), P("dp", "tensor"), P(("dp", "tensor"), None))
    out_specs = (P(("dp", "tensor"), None), P("dp", "tensor"), P("dp", "tensor"))
    return jax.shard_map(body, mesh=mesh, in_specs=in_specs, out_specs=out_specs, check_vma=False)
```

```python
import jax
import jax.numpy as jnp
from jax import lax
from jax.experimental import pallas as pl
from jax.experimental.pallas import tpu as pltpu
from jax.sharding import PartitionSpec as P

NX, NY, NL, NH = 4, 8, 3, 4
SUBS_G = 3
N_COPIES = 128
VMEM_MIB = 60
F32 = jnp.float32
BF16 = jnp.bfloat16


def kernel(
    x_hbm, w_ref, c_hbm,
    key_ref, grad_hbm, wg_ref,
    x_v, wz, wa, wb, wall, wabs, cot, part, part_in, key_a, key_b, g, a_half, a_in, ax_in, bx_a, bx_in, b_sum, b_half, b_in, gz, grad_v,
    send_sems, recv_sems, local_sems,
):
    dp = lax.axis_index("dp")
    tn = lax.axis_index("tensor")
    x = dp % NX
    zl = (dp // NX) % NL
    y = dp // (NX * NL)
    core = tn % 2
    zh = tn // 2

    def at(x=x, zl=zl, y=y, zh=zh, core=core):
        return ((y * NL + zl) * NX + x, zh * 2 + core)

    y_up, y_down = (y + 1) % NY, (y + NY - 1) % NY
    h_up, h_down, h_far = (zh + 1) % NH, (zh + NH - 1) % NH, (zh + 2) % NH
    to_yup, to_ydown = at(y=y_up), at(y=y_down)
    x_up, x_down, x_far = (x + 1) % NX, (x + NX - 1) % NX, (x + 2) % NX
    to_xup, to_xdown = at(x=x_up), at(x=x_down)
    to_hup, to_hdown = at(zh=h_up), at(zh=h_down)
    sibling = at(core=1 - core)

    used = [0]
    sends = []

    def send(src, dst, where):
        n = used[0]
        used[0] += 1
        copy = pltpu.make_async_remote_copy(
            src_ref=src, dst_ref=dst, send_sem=send_sems.at[n], recv_sem=recv_sems.at[n],
            device_id=where, device_id_type=pl.DeviceIdType.MESH,
        )
        copy.start()
        sends.append(copy)
        return copy

    load_x = pltpu.make_async_copy(x_hbm, x_v, local_sems.at[0])
    load_x.start()
    load_c = pltpu.make_async_copy(c_hbm, cot.at[tn], local_sems.at[1])
    load_c.start()
    w32 = w_ref[...].astype(F32)
    for half in range(2):
        quarters = [w32[:, 512 * half + 256 * n : 512 * half + 256 * n + 256] for n in range(2)]
        wz[zl, half] = jnp.concatenate(quarters, axis=0).astype(BF16)

    barrier = pltpu.get_barrier_semaphore()
    partners = [at(x=(x + d) % NX) for d in range(1, NX)]
    partners += [at(zl=(zl + d) % NL) for d in range(1, NL)]
    partners += [to_yup, to_ydown, to_hup, to_hdown, sibling]
    for partner in partners:
        pl.semaphore_signal(barrier, inc=1, device_id=partner, device_id_type=pl.DeviceIdType.MESH)
    pl.semaphore_wait(barrier, len(partners))

    w_z = [send(wz.at[zl], wz.at[zl], at(zl=(zl + d) % NL)) for d in range(1, NL)]
    load_c.wait()
    c_up = send(cot.at[tn], cot.at[tn], to_hup)
    c_down = send(cot.at[tn], cot.at[tn], to_hdown)
    c_sib = [send(cot.at[tn], cot.at[tn], sibling)]
    for copy in w_z:
        copy.wait_recv()

    wa[1, x] = wz[:, 0]
    wa_x = [send(wz.at[:, 0], wa.at[1, x], at(x=(x + d) % NX)) for d in range(1, NX)]

    def wa_step(k, before):
        new = []
        for q in range(2):
            for side, place, there, where in ((0, 1 - k, -k, to_yup), (1, 1 + k, 2 + k, to_ydown)):
                if k == 3 and q != side:
                    continue
                if before:
                    before[2 * q + side].wait_recv()
                xs = pl.ds(2 * q, 2)
                new.append(send(wa.at[place % NY, xs], wa.at[there % NY, xs], where))
        return new

    def wb_step(k, before):
        new = []
        for side, place, there, where in ((0, 1 - k, -k, to_yup), (1, 1 + k, 2 + k, to_ydown)):
            if before:
                before[side].wait_recv()
            src, dst = (wb.at[x, i % NY] for i in (place, there))
            if k == 3:
                lanes = pl.ds(128 * side, 128)
                src, dst = src.at[:, :, lanes], dst.at[:, :, lanes]
            new.append(send(src, dst, where))
        return new

    def wb_along_x(n):
        block = wb.at[x, pl.ds(4 * n, 4)]
        return send(block, block, to_xup), send(block, block, to_xdown)

    def wait(copies):
        for copy in copies:
            copy.wait_recv()

    wb[x, 1] = wz[:, 1]
    b_ring = wb_step(0, None)
    b_ring = wb_step(1, b_ring)
    wait(wa_x)
    a_ring = wa_step(0, None)
    wait(b_ring)
    b_x0 = wb_along_x(0)
    b_ring = wb_step(2, None)
    b_ring = wb_step(3, b_ring)
    a_ring = wa_step(1, a_ring)
    b_x0[0].wait_recv()
    block = wb.at[x_down, pl.ds(0, 4)]
    b_far0 = send(block, block, to_xup)
    wait(b_ring)
    b_x1 = wb_along_x(1)
    a_ring = wa_step(2, a_ring)

    lo, hi = pl.ds(0, 64), pl.ds(64, 64)
    c_up.wait_recv()
    from_down = cot.at[h_down * 2 + core]
    c_far0 = send(from_down.at[lo], from_down.at[lo], to_hup)
    c_down.wait_recv()
    from_up = cot.at[h_up * 2 + core]
    c_far1 = send(from_up.at[hi], from_up.at[hi], to_hdown)
    c_sib.append(send(from_down, from_down, sibling))
    c_sib.append(send(from_up, from_up, sibling))

    b_x1[1].wait_recv()
    block = wb.at[x_up, pl.ds(4, 4)]
    b_far1 = send(block, block, to_xdown)
    a_last = wa_step(3, a_ring)
    wait((a_ring[1], a_ring[2]))

    def assemble(n):
        for place in range(4 * n, 4 * n + 4):
            for run in range(NL):
                for half, src in ((0, wa[place, :, run]), (1, wb[:, place, run])):
                    wide = src.astype(F32)
                    for quarter in range(2):
                        rows = wide[:, 8 * quarter : 8 * quarter + 8].reshape(32, 256).astype(BF16)
                        at_lane = 512 * half + 256 * quarter
                        wall[place * NL + run, :, at_lane : at_lane + 256] = rows

    def key_product(n):
        out = []
        for j, h in enumerate((h_far, h_up, h_down, zh)):
            rows = pl.ds(pl.multiple_of(h * 256, 256), 256)
            prod = lax.dot_general(
                x_v[rows, :], wall[12 * n : 12 * n + 12].reshape(384, 1024), (((1,), (1,)), ((), ())),
                preferred_element_type=F32,
            )
            part[n, j] = prod.reshape(2, 128, 384)
            out.append(send(part.at[n, j, 1 - core], part_in.at[n, j], sibling))
        return out

    def key_first(n, halves):
        def join(j):
            halves[j].wait_recv()
            part[n, j, core] = part[n, j, core] + part_in[n, j]

        join(0)
        a0 = send(part.at[n, 0, core, lo], key_a.at[n, 0], to_hup)
        a1 = send(part.at[n, 0, core, hi], key_a.at[n, 1], to_hdown)
        join(1)
        b = [send(part.at[n, 1, core, hi], key_b.at[n, 0, hi], to_hup)]
        join(2)
        b.append(send(part.at[n, 2, core, lo], key_b.at[n, 1, lo], to_hdown))
        join(3)
        return a0, a1, b

    def key_relay(n, flows):
        a0, a1, b = flows
        a0.wait_recv()
        part[n, 1, core, lo] = part[n, 1, core, lo] + key_a[n, 0]
        b.append(send(part.at[n, 1, core, lo], key_b.at[n, 0, lo], to_hup))
        a1.wait_recv()
        part[n, 2, core, hi] = part[n, 2, core, hi] + key_a[n, 1]
        b.append(send(part.at[n, 2, core, hi], key_b.at[n, 1, hi], to_hdown))
        return b

    load_x.wait()
    wait((b_x0[1], b_far0))
    assemble(0)
    halves0 = key_product(0)
    wait((b_x1[0], b_far1))
    wait(a_last)
    flows0 = key_first(0, halves0)
    assemble(1)
    halves = key_product(1)

    c_far0.wait_recv()
    c_far1.wait_recv()
    far = cot.at[h_far * 2 + core]
    c_sib.append(send(far, far, sibling))
    flows1 = key_first(1, halves)
    for copy in c_sib:
        copy.wait_recv()

    for q in range(3):
        left = cot[:, :, 256 * q : 256 * q + 256].reshape(1024, 256)
        prod = lax.dot_general(left, x_v[...], (((0,), (0,)), ((), ())), preferred_element_type=F32)
        g[8 * q : 8 * q + 8] = prod.reshape(8, 32, 1024)

    fa, fb = pl.ds(0, 512), pl.ds(512, 512)
    size = NL // SUBS_G

    def a_first(q):
        far_y = ((y + 4) % NY) * NL + q * size
        at_q = pl.ds(q * size, size)
        a = send(g.at[pl.ds(far_y, size), pl.ds(0, 16), fa], a_half.at[0, at_q], to_yup)
        b = send(g.at[pl.ds(far_y, size), pl.ds(16, 16), fa], a_half.at[1, at_q], to_ydown)
        return a, b

    def a_step(k, q, before):
        at_q = pl.ds(q * size, size)
        up = ((y + 4 - k) % NY) * NL + q * size
        down = ((y + 4 + k) % NY) * NL + q * size
        new = []
        for side, block, where in ((0, up, to_yup), (1, down, to_ydown)):
            before[side].wait_recv()
            here = pl.ds(block, size)
            if k == 1:
                rows = pl.ds(16 * side, 16)
                g[here, rows, fa] = g[here, rows, fa] + a_half[side, at_q]
            else:
                g[here, :, fa] = g[here, :, fa] + a_in[side, k - 2, at_q]
            new.append(send(g.at[here, :, fa], a_in.at[side, k - 1, at_q], where))
        return new

    first, last = pl.ds(0, 12), pl.ds(12, 12)

    def rows_of(to):
        return pl.ds(pl.multiple_of(to * 8, 8), 8)

    a_flow = [a_first(q) for q in range(SUBS_G)]
    g_far0 = send(g.at[first, rows_of(x_far), fb], bx_a.at[0], to_xup)
    g_far1 = send(g.at[last, rows_of(x_far), fb], bx_a.at[1], to_xdown)
    g_x = [
        send(g.at[last, rows_of(x_up), fb], bx_in.at[0, last], to_xup),
        send(g.at[first, rows_of(x_down), fb], bx_in.at[1, first], to_xdown),
    ]

    for place in range(NY):
        wabs[pl.ds(((y + NY - 1 + place) % NY) * NL, NL)] = wall[NL * place : NL * place + NL]

    def grad_chunk(i):
        prod = jnp.dot(
            cot[2 * i : 2 * i + 2].reshape(256, 768), wabs[...].reshape(768, 1024), preferred_element_type=F32
        )
        grad_v[256 * i : 256 * i + 256] = prod.astype(BF16)

    grad_chunk(0)
    grad_chunk(1)
    for q in range(SUBS_G):
        a_flow[q] = a_step(1, q, a_flow[q])
    g_far0.wait_recv()
    g[first, rows_of(x_up), fb] = g[first, rows_of(x_up), fb] + bx_a[0]
    g_x.append(send(g.at[first, rows_of(x_up), fb], bx_in.at[0, first], to_xup))
    g_far1.wait_recv()
    g[last, rows_of(x_down), fb] = g[last, rows_of(x_down), fb] + bx_a[1]
    g_x.append(send(g.at[last, rows_of(x_down), fb], bx_in.at[1, last], to_xdown))
    k_b0 = key_relay(0, flows0)
    grad_chunk(2)
    grad_chunk(3)
    store_grad = pltpu.make_async_copy(grad_v, grad_hbm, local_sems.at[2])
    store_grad.start()
    for q in range(SUBS_G):
        a_flow[q] = a_step(2, q, a_flow[q])

    for copy in g_x:
        copy.wait_recv()
    b_sum[...] = g[:, rows_of(x), fb] + (bx_in[0] + bx_in[1])

    def b_step(k, before):
        new = []
        for side, place, where in ((0, y + 4 - k, to_yup), (1, y + 4 + k, to_ydown)):
            here = pl.ds((place % NY) * NL, NL)
            lanes = pl.ds(256 * side, 256)
            if k > 0:
                before[side].wait_recv()
            if k == 0:
                new.append(send(b_sum.at[here, :, lanes], b_half.at[side], where))
                continue
            if k == 1:
                b_sum[here, :, lanes] = b_sum[here, :, lanes] + b_half[side]
            else:
                b_sum[here] = b_sum[here] + b_in[side, k - 2]
            new.append(send(b_sum.at[here], b_in.at[side, k - 1], where))
        return new

    b_flow = b_step(0, None)
    for q in range(SUBS_G):
        a_flow[q] = a_step(3, q, a_flow[q])
    b_flow = b_step(1, b_flow)
    k_b1 = key_relay(1, flows1)
    b_flow = b_step(2, b_flow)
    b_flow = b_step(3, b_flow)
    for q in range(SUBS_G):
        a_flow[q][0].wait_recv()
        a_flow[q][1].wait_recv()
    own = pl.ds(y * NL, NL)
    g[own, :, fa] = g[own, :, fa] + (a_in[0, 2] + a_in[1, 2])
    a_x = []
    for d in range(1, NX):
        to = (x + d) % NX
        a_x.append(send(g.at[own, rows_of(to), fa], ax_in.at[x], at(x=to)))
    ax_in[x] = g[own, rows_of(x), fa]
    for copy in b_flow:
        copy.wait_recv()
    gz[pl.ds(3, 3), :, fb] = b_sum[own] + (b_in[0, 2] + b_in[1, 2])
    for copy in a_x:
        copy.wait_recv()
    gz[pl.ds(3, 3), :, fa] = (ax_in[0] + ax_in[1]) + (ax_in[2] + ax_in[3])

    g_z = []
    for d in range(1, NL):
        to = (zl + d) % NL
        g_z.append(send(gz.at[3 + to], gz.at[d], at(zl=to)))

    turn = ((y + NY - 1) % NY) * 96
    gap = lax.broadcasted_iota(jnp.int32, (768, 768), 1) - lax.broadcasted_iota(jnp.int32, (768, 768), 0)
    back = jnp.where((gap == turn) | (gap == turn - 768), 1.0, 0.0).astype(BF16)
    keys = None
    for n, copies in ((0, k_b0), (1, k_b1)):
        for copy in copies:
            copy.wait_recv()
        rel = (part[n, 3, core] + (key_b[n, 0] + key_b[n, 1])).astype(BF16)
        term = jnp.dot(rel, back[384 * n : 384 * n + 384], preferred_element_type=F32)
        keys = term if keys is None else keys + term
    key_ref[...] = keys.astype(BF16)

    for copy in g_z:
        copy.wait_recv()
    wg_ref[...] = gz[3 + zl] + gz[1] + gz[2]

    for copy in sends:
        copy.wait_send()
    store_grad.wait()


def body(inputs, key_weight, key_cotangent):
    vmem = pl.BlockSpec(memory_space=pltpu.VMEM)
    hbm = pl.BlockSpec(memory_space=pl.ANY)
    return pl.pallas_call(
        kernel,
        out_shape=(
            jax.ShapeDtypeStruct((128, 768), BF16),
            jax.ShapeDtypeStruct((1024, 1024), BF16),
            jax.ShapeDtypeStruct((8, 1024), F32),
        ),
        in_specs=[hbm, vmem, hbm],
        out_specs=(vmem, hbm, vmem),
        scratch_shapes=[
            pltpu.VMEM((1024, 1024), BF16),
            pltpu.VMEM((NL, 2, 16, 256), BF16),
            pltpu.VMEM((NY, NX, NL, 16, 256), BF16),
            pltpu.VMEM((NX, NY, NL, 16, 256), BF16),
            pltpu.VMEM((24, 32, 1024), BF16),
            pltpu.VMEM((24, 32, 1024), BF16),
            pltpu.VMEM((8, 128, 768), BF16),
            pltpu.VMEM((2, 4, 2, 128, 384), F32),
            pltpu.VMEM((2, 4, 128, 384), F32),
            pltpu.VMEM((2, 2, 64, 384), F32),
            pltpu.VMEM((2, 2, 128, 384), F32),
            pltpu.VMEM((24, 32, 1024), F32),
            pltpu.VMEM((2, 3, 16, 512), F32),
            pltpu.VMEM((2, 3, 3, 32, 512), F32),
            pltpu.VMEM((NX, NL, 8, 512), F32),
            pltpu.VMEM((2, 12, 8, 512), F32),
            pltpu.VMEM((2, 24, 8, 512), F32),
            pltpu.VMEM((24, 8, 512), F32),
            pltpu.VMEM((2, 3, 8, 256), F32),
            pltpu.VMEM((2, 3, 3, 8, 512), F32),
            pltpu.VMEM((6, 8, 1024), F32),
            pltpu.VMEM((1024, 1024), BF16),
            pltpu.SemaphoreType.DMA((N_COPIES,)),
            pltpu.SemaphoreType.DMA((N_COPIES,)),
            pltpu.SemaphoreType.DMA((3,)),
        ],
        compiler_params=pltpu.CompilerParams(
            collective_id=0, has_side_effects=True, vmem_limit_bytes=VMEM_MIB * 1024 * 1024
        ),
        cost_estimate=pl.CostEstimate(flops=4_831_838_208, bytes_accessed=5_000_000, transcendentals=0),
    )(inputs, key_weight, key_cotangent)


def solution(mesh):
    in_specs = (P("dp", "tensor"), P("dp", "tensor"), P(("dp", "tensor"), None))
    out_specs = (P(("dp", "tensor"), None), P("dp", "tensor"), P("dp", "tensor"))
    return jax.shard_map(body, mesh=mesh, in_specs=in_specs, out_specs=out_specs, check_vma=False)
```

```python
import jax
import jax.numpy as jnp
from jax import lax
from jax.experimental import pallas as pl
from jax.experimental.pallas import tpu as pltpu
from jax.sharding import PartitionSpec as P

NX, NY, NL, NH = 4, 8, 3, 4
SUBS_G = 3
N_COPIES = 128
VMEM_MIB = 60
F32 = jnp.float32
BF16 = jnp.bfloat16


def kernel(
    x_hbm, w_ref, c_hbm,
    key_ref, grad_hbm, wg_ref,
    x_v, wz, wa, wb, wall, wabs, cot, part, part_in, key_a, key_b, g, a_half, a_in, ax_in, bx_a, bx_in, b_sum, b_half, b_in, gz, grad_v,
    send_sems, recv_sems, local_sems,
):
    dp = lax.axis_index("dp")
    tn = lax.axis_index("tensor")
    x = dp % NX
    zl = (dp // NX) % NL
    y = dp // (NX * NL)
    core = tn % 2
    zh = tn // 2

    def at(x=x, zl=zl, y=y, zh=zh, core=core):
        return ((y * NL + zl) * NX + x, zh * 2 + core)

    y_up, y_down = (y + 1) % NY, (y + NY - 1) % NY
    h_up, h_down, h_far = (zh + 1) % NH, (zh + NH - 1) % NH, (zh + 2) % NH
    to_yup, to_ydown = at(y=y_up), at(y=y_down)
    x_up, x_down, x_far = (x + 1) % NX, (x + NX - 1) % NX, (x + 2) % NX
    to_xup, to_xdown = at(x=x_up), at(x=x_down)
    to_hup, to_hdown = at(zh=h_up), at(zh=h_down)
    sibling = at(core=1 - core)

    used = [0]
    sends = []

    def send(src, dst, where):
        n = used[0]
        used[0] += 1
        copy = pltpu.make_async_remote_copy(
            src_ref=src, dst_ref=dst, send_sem=send_sems.at[n], recv_sem=recv_sems.at[n],
            device_id=where, device_id_type=pl.DeviceIdType.MESH,
        )
        copy.start()
        sends.append(copy)
        return copy

    load_x = pltpu.make_async_copy(x_hbm, x_v, local_sems.at[0])
    load_x.start()
    load_c = pltpu.make_async_copy(c_hbm, cot.at[tn], local_sems.at[1])
    load_c.start()
    w32 = w_ref[...].astype(F32)
    for half in range(2):
        quarters = [w32[:, 512 * half + 256 * n : 512 * half + 256 * n + 256] for n in range(2)]
        wz[zl, half] = jnp.concatenate(quarters, axis=0).astype(BF16)

    barrier = pltpu.get_barrier_semaphore()
    partners = [at(x=(x + d) % NX) for d in range(1, NX)]
    partners += [at(zl=(zl + d) % NL) for d in range(1, NL)]
    partners += [to_yup, to_ydown, to_hup, to_hdown, sibling]
    for partner in partners:
        pl.semaphore_signal(barrier, inc=1, device_id=partner, device_id_type=pl.DeviceIdType.MESH)
    pl.semaphore_wait(barrier, len(partners))

    w_z = [send(wz.at[zl], wz.at[zl], at(zl=(zl + d) % NL)) for d in range(1, NL)]
    load_c.wait()
    c_up = send(cot.at[tn], cot.at[tn], to_hup)
    c_down = send(cot.at[tn], cot.at[tn], to_hdown)
    c_sib = [send(cot.at[tn], cot.at[tn], sibling)]
    for copy in w_z:
        copy.wait_recv()

    wa[1, x] = wz[:, 0]
    wa_x = [send(wz.at[:, 0], wa.at[1, x], at(x=(x + d) % NX)) for d in range(1, NX)]

    def wa_step(k, before):
        new = []
        for q in range(2):
            for side, place, there, where in ((0, 1 - k, -k, to_yup), (1, 1 + k, 2 + k, to_ydown)):
                if k == 3 and q != side:
                    continue
                if before:
                    before[2 * q + side].wait_recv()
                xs = pl.ds(2 * q, 2)
                new.append(send(wa.at[place % NY, xs], wa.at[there % NY, xs], where))
        return new

    def wb_step(k, before):
        new = []
        for side, place, there, where in ((0, 1 - k, -k, to_yup), (1, 1 + k, 2 + k, to_ydown)):
            if before:
                before[side].wait_recv()
            src, dst = (wb.at[x, i % NY] for i in (place, there))
            if k == 3:
                lanes = pl.ds(128 * side, 128)
                src, dst = src.at[:, :, lanes], dst.at[:, :, lanes]
            new.append(send(src, dst, where))
        return new

    def wb_along_x(n):
        block = wb.at[x, pl.ds(4 * n, 4)]
        return send(block, block, to_xup), send(block, block, to_xdown)

    def wait(copies):
        for copy in copies:
            copy.wait_recv()

    wb[x, 1] = wz[:, 1]
    b_ring = wb_step(0, None)
    b_ring = wb_step(1, b_ring)
    wait(wa_x)
    a_ring = wa_step(0, None)
    wait(b_ring)
    b_x0 = wb_along_x(0)
    b_ring = wb_step(2, None)
    b_ring = wb_step(3, b_ring)
    a_ring = wa_step(1, a_ring)
    b_x0[0].wait_recv()
    block = wb.at[x_down, pl.ds(0, 4)]
    b_far0 = send(block, block, to_xup)
    wait(b_ring)
    b_x1 = wb_along_x(1)
    a_ring = wa_step(2, a_ring)

    lo, hi = pl.ds(0, 64), pl.ds(64, 64)
    c_up.wait_recv()
    from_down = cot.at[h_down * 2 + core]
    c_far0 = send(from_down.at[lo], from_down.at[lo], to_hup)
    c_down.wait_recv()
    from_up = cot.at[h_up * 2 + core]
    c_far1 = send(from_up.at[hi], from_up.at[hi], to_hdown)
    c_sib.append(send(from_down, from_down, sibling))
    c_sib.append(send(from_up, from_up, sibling))

    b_x1[1].wait_recv()
    block = wb.at[x_up, pl.ds(4, 4)]
    b_far1 = send(block, block, to_xdown)
    a_last = wa_step(3, a_ring)
    wait((a_ring[1], a_ring[2]))

    def assemble(n):
        for place in range(4 * n, 4 * n + 4):
            for run in range(NL):
                for half, src in ((0, wa[place, :, run]), (1, wb[:, place, run])):
                    wide = src.astype(F32)
                    for quarter in range(2):
                        rows = wide[:, 8 * quarter : 8 * quarter + 8].reshape(32, 256).astype(BF16)
                        at_lane = 512 * half + 256 * quarter
                        wall[place * NL + run, :, at_lane : at_lane + 256] = rows

    def key_product(n):
        out = []
        for j, h in enumerate((h_far, h_up, h_down, zh)):
            rows = pl.ds(pl.multiple_of(h * 256, 256), 256)
            prod = lax.dot_general(
                x_v[rows, :], wall[12 * n : 12 * n + 12].reshape(384, 1024), (((1,), (1,)), ((), ())),
                preferred_element_type=F32,
            )
            part[n, j] = prod.reshape(2, 128, 384)
            out.append(send(part.at[n, j, 1 - core], part_in.at[n, j], sibling))
        return out

    def key_first(n, halves):
        def join(j):
            halves[j].wait_recv()
            part[n, j, core] = part[n, j, core] + part_in[n, j]

        join(0)
        a0 = send(part.at[n, 0, core, lo], key_a.at[n, 0], to_hup)
        a1 = send(part.at[n, 0, core, hi], key_a.at[n, 1], to_hdown)
        join(1)
        b = [send(part.at[n, 1, core, hi], key_b.at[n, 0, hi], to_hup)]
        join(2)
        b.append(send(part.at[n, 2, core, lo], key_b.at[n, 1, lo], to_hdown))
        join(3)
        return a0, a1, b

    def key_relay(n, flows):
        a0, a1, b = flows
        a0.wait_recv()
        part[n, 1, core, lo] = part[n, 1, core, lo] + key_a[n, 0]
        b.append(send(part.at[n, 1, core, lo], key_b.at[n, 0, lo], to_hup))
        a1.wait_recv()
        part[n, 2, core, hi] = part[n, 2, core, hi] + key_a[n, 1]
        b.append(send(part.at[n, 2, core, hi], key_b.at[n, 1, hi], to_hdown))
        return b

    load_x.wait()
    wait((b_x0[1], b_far0))
    assemble(0)
    halves = key_product(0)
    c_far0.wait_recv()
    c_far1.wait_recv()
    far = cot.at[h_far * 2 + core]
    c_sib.append(send(far, far, sibling))
    flows0 = key_first(0, halves)
    wait(c_sib)

    def grad_product(half):
        lanes = pl.ds(512 * half, 512)
        for q in range(3):
            left = cot[:, :, 256 * q : 256 * q + 256].reshape(1024, 256)
            prod = lax.dot_general(left, x_v[:, lanes], (((0,), (0,)), ((), ())), preferred_element_type=F32)
            g[8 * q : 8 * q + 8, :, lanes] = prod.reshape(8, 32, 512)

    fa, fb = pl.ds(0, 512), pl.ds(512, 512)
    size = NL // SUBS_G

    def a_first(q):
        far_y = ((y + 4) % NY) * NL + q * size
        at_q = pl.ds(q * size, size)
        a = send(g.at[pl.ds(far_y, size), pl.ds(0, 16), fa], a_half.at[0, at_q], to_yup)
        b = send(g.at[pl.ds(far_y, size), pl.ds(16, 16), fa], a_half.at[1, at_q], to_ydown)
        return a, b

    def a_step(k, q, before):
        at_q = pl.ds(q * size, size)
        up = ((y + 4 - k) % NY) * NL + q * size
        down = ((y + 4 + k) % NY) * NL + q * size
        new = []
        for side, block, where in ((0, up, to_yup), (1, down, to_ydown)):
            before[side].wait_recv()
            here = pl.ds(block, size)
            if k == 1:
                rows = pl.ds(16 * side, 16)
                g[here, rows, fa] = g[here, rows, fa] + a_half[side, at_q]
            else:
                g[here, :, fa] = g[here, :, fa] + a_in[side, k - 2, at_q]
            new.append(send(g.at[here, :, fa], a_in.at[side, k - 1, at_q], where))
        return new

    first, last = pl.ds(0, 12), pl.ds(12, 12)

    def rows_of(to):
        return pl.ds(pl.multiple_of(to * 8, 8), 8)

    grad_product(1)
    g_far0 = send(g.at[first, rows_of(x_far), fb], bx_a.at[0], to_xup)
    g_far1 = send(g.at[last, rows_of(x_far), fb], bx_a.at[1], to_xdown)
    g_x = [
        send(g.at[last, rows_of(x_up), fb], bx_in.at[0, last], to_xup),
        send(g.at[first, rows_of(x_down), fb], bx_in.at[1, first], to_xdown),
    ]

    grad_product(0)
    a_flow = [a_first(q) for q in range(SUBS_G)]

    wait((b_x1[0], b_far1))
    wait(a_last)
    assemble(1)
    flows1 = key_first(1, key_product(1))

    def grad_chunk(i):
        prod = jnp.dot(
            cot[2 * i : 2 * i + 2].reshape(256, 768), wabs[...].reshape(768, 1024), preferred_element_type=F32
        )
        grad_v[256 * i : 256 * i + 256] = prod.astype(BF16)

    for q in range(SUBS_G):
        a_flow[q] = a_step(1, q, a_flow[q])
    g_far0.wait_recv()
    g[first, rows_of(x_up), fb] = g[first, rows_of(x_up), fb] + bx_a[0]
    g_x.append(send(g.at[first, rows_of(x_up), fb], bx_in.at[0, first], to_xup))
    g_far1.wait_recv()
    g[last, rows_of(x_down), fb] = g[last, rows_of(x_down), fb] + bx_a[1]
    g_x.append(send(g.at[last, rows_of(x_down), fb], bx_in.at[1, last], to_xdown))
    k_b0 = key_relay(0, flows0)
    for place in range(NY):
        wabs[pl.ds(((y + NY - 1 + place) % NY) * NL, NL)] = wall[NL * place : NL * place + NL]
    grad_chunk(0)
    grad_chunk(1)
    for q in range(SUBS_G):
        a_flow[q] = a_step(2, q, a_flow[q])
    grad_chunk(2)
    grad_chunk(3)
    store_grad = pltpu.make_async_copy(grad_v, grad_hbm, local_sems.at[2])
    store_grad.start()

    for copy in g_x:
        copy.wait_recv()
    b_sum[...] = g[:, rows_of(x), fb] + (bx_in[0] + bx_in[1])

    def b_step(k, before):
        new = []
        for side, place, where in ((0, y + 4 - k, to_yup), (1, y + 4 + k, to_ydown)):
            here = pl.ds((place % NY) * NL, NL)
            lanes = pl.ds(256 * side, 256)
            if k > 0:
                before[side].wait_recv()
            if k == 0:
                new.append(send(b_sum.at[here, :, lanes], b_half.at[side], where))
                continue
            if k == 1:
                b_sum[here, :, lanes] = b_sum[here, :, lanes] + b_half[side]
            else:
                b_sum[here] = b_sum[here] + b_in[side, k - 2]
            new.append(send(b_sum.at[here], b_in.at[side, k - 1], where))
        return new

    b_flow = b_step(0, None)
    for q in range(SUBS_G):
        a_flow[q] = a_step(3, q, a_flow[q])
    b_flow = b_step(1, b_flow)
    k_b1 = key_relay(1, flows1)
    b_flow = b_step(2, b_flow)
    b_flow = b_step(3, b_flow)
    for q in range(SUBS_G):
        a_flow[q][0].wait_recv()
        a_flow[q][1].wait_recv()
    own = pl.ds(y * NL, NL)
    g[own, :, fa] = g[own, :, fa] + (a_in[0, 2] + a_in[1, 2])
    a_x = []
    for d in range(1, NX):
        to = (x + d) % NX
        a_x.append(send(g.at[own, rows_of(to), fa], ax_in.at[x], at(x=to)))
    ax_in[x] = g[own, rows_of(x), fa]
    for copy in b_flow:
        copy.wait_recv()
    gz[pl.ds(3, 3), :, fb] = b_sum[own] + (b_in[0, 2] + b_in[1, 2])
    for copy in a_x:
        copy.wait_recv()
    gz[pl.ds(3, 3), :, fa] = (ax_in[0] + ax_in[1]) + (ax_in[2] + ax_in[3])

    g_z = []
    for d in range(1, NL):
        to = (zl + d) % NL
        g_z.append(send(gz.at[3 + to], gz.at[d], at(zl=to)))

    turn = ((y + NY - 1) % NY) * 96
    gap = lax.broadcasted_iota(jnp.int32, (768, 768), 1) - lax.broadcasted_iota(jnp.int32, (768, 768), 0)
    back = jnp.where((gap == turn) | (gap == turn - 768), 1.0, 0.0).astype(BF16)
    keys = None
    for n, copies in ((0, k_b0), (1, k_b1)):
        for copy in copies:
            copy.wait_recv()
        rel = (part[n, 3, core] + (key_b[n, 0] + key_b[n, 1])).astype(BF16)
        term = jnp.dot(rel, back[384 * n : 384 * n + 384], preferred_element_type=F32)
        keys = term if keys is None else keys + term
    key_ref[...] = keys.astype(BF16)

    for copy in g_z:
        copy.wait_recv()
    wg_ref[...] = gz[3 + zl] + gz[1] + gz[2]

    for copy in sends:
        copy.wait_send()
    store_grad.wait()


def body(inputs, key_weight, key_cotangent):
    vmem = pl.BlockSpec(memory_space=pltpu.VMEM)
    hbm = pl.BlockSpec(memory_space=pl.ANY)
    return pl.pallas_call(
        kernel,
        out_shape=(
            jax.ShapeDtypeStruct((128, 768), BF16),
            jax.ShapeDtypeStruct((1024, 1024), BF16),
            jax.ShapeDtypeStruct((8, 1024), F32),
        ),
        in_specs=[hbm, vmem, hbm],
        out_specs=(vmem, hbm, vmem),
        scratch_shapes=[
            pltpu.VMEM((1024, 1024), BF16),
            pltpu.VMEM((NL, 2, 16, 256), BF16),
            pltpu.VMEM((NY, NX, NL, 16, 256), BF16),
            pltpu.VMEM((NX, NY, NL, 16, 256), BF16),
            pltpu.VMEM((24, 32, 1024), BF16),
            pltpu.VMEM((24, 32, 1024), BF16),
            pltpu.VMEM((8, 128, 768), BF16),
            pltpu.VMEM((2, 4, 2, 128, 384), F32),
            pltpu.VMEM((2, 4, 128, 384), F32),
            pltpu.VMEM((2, 2, 64, 384), F32),
            pltpu.VMEM((2, 2, 128, 384), F32),
            pltpu.VMEM((24, 32, 1024), F32),
            pltpu.VMEM((2, 3, 16, 512), F32),
            pltpu.VMEM((2, 3, 3, 32, 512), F32),
            pltpu.VMEM((NX, NL, 8, 512), F32),
            pltpu.VMEM((2, 12, 8, 512), F32),
            pltpu.VMEM((2, 24, 8, 512), F32),
            pltpu.VMEM((24, 8, 512), F32),
            pltpu.VMEM((2, 3, 8, 256), F32),
            pltpu.VMEM((2, 3, 3, 8, 512), F32),
            pltpu.VMEM((6, 8, 1024), F32),
            pltpu.VMEM((1024, 1024), BF16),
            pltpu.SemaphoreType.DMA((N_COPIES,)),
            pltpu.SemaphoreType.DMA((N_COPIES,)),
            pltpu.SemaphoreType.DMA((3,)),
        ],
        compiler_params=pltpu.CompilerParams(
            collective_id=0, has_side_effects=True, vmem_limit_bytes=VMEM_MIB * 1024 * 1024
        ),
        cost_estimate=pl.CostEstimate(flops=4_831_838_208, bytes_accessed=5_000_000, transcendentals=0),
    )(inputs, key_weight, key_cotangent)


def solution(mesh):
    in_specs = (P("dp", "tensor"), P("dp", "tensor"), P(("dp", "tensor"), None))
    out_specs = (P(("dp", "tensor"), None), P("dp", "tensor"), P("dp", "tensor"))
    return jax.shard_map(body, mesh=mesh, in_specs=in_specs, out_specs=out_specs, check_vma=False)
```

```python
import jax
import jax.numpy as jnp
from jax import lax
from jax.experimental import pallas as pl
from jax.experimental.pallas import tpu as pltpu
from jax.sharding import PartitionSpec as P

NX, NY, NL, NH = 4, 8, 3, 4
SUBS_G = 3
N_COPIES = 128
VMEM_MIB = 60
F32 = jnp.float32
BF16 = jnp.bfloat16


def kernel(
    x_hbm, w_ref, c_hbm,
    key_ref, grad_hbm, wg_ref,
    x_v, wz, wa, wb, wall, wabs, cot, part, part_in, key_a, key_b, g, a_half, a_in, ax_in, bx_a, bx_in, b_sum, b_half, b_in, gz, grad_v,
    send_sems, recv_sems, local_sems,
):
    dp = lax.axis_index("dp")
    tn = lax.axis_index("tensor")
    x = dp % NX
    zl = (dp // NX) % NL
    y = dp // (NX * NL)
    core = tn % 2
    zh = tn // 2

    def at(x=x, zl=zl, y=y, zh=zh, core=core):
        return ((y * NL + zl) * NX + x, zh * 2 + core)

    y_up, y_down = (y + 1) % NY, (y + NY - 1) % NY
    h_up, h_down, h_far = (zh + 1) % NH, (zh + NH - 1) % NH, (zh + 2) % NH
    to_yup, to_ydown = at(y=y_up), at(y=y_down)
    x_up, x_down, x_far = (x + 1) % NX, (x + NX - 1) % NX, (x + 2) % NX
    to_xup, to_xdown = at(x=x_up), at(x=x_down)
    to_hup, to_hdown = at(zh=h_up), at(zh=h_down)
    sibling = at(core=1 - core)

    used = [0]
    sends = []

    def send(src, dst, where):
        n = used[0]
        used[0] += 1
        copy = pltpu.make_async_remote_copy(
            src_ref=src, dst_ref=dst, send_sem=send_sems.at[n], recv_sem=recv_sems.at[n],
            device_id=where, device_id_type=pl.DeviceIdType.MESH,
        )
        copy.start()
        sends.append(copy)
        return copy

    load_x = pltpu.make_async_copy(x_hbm, x_v, local_sems.at[0])
    load_x.start()
    load_c = pltpu.make_async_copy(c_hbm, cot.at[tn], local_sems.at[1])
    load_c.start()
    w32 = w_ref[...].astype(F32)
    for half in range(2):
        quarters = [w32[:, 512 * half + 256 * n : 512 * half + 256 * n + 256] for n in range(2)]
        wz[zl, half] = jnp.concatenate(quarters, axis=0).astype(BF16)

    barrier = pltpu.get_barrier_semaphore()
    partners = [at(x=(x + d) % NX) for d in range(1, NX)]
    partners += [at(zl=(zl + d) % NL) for d in range(1, NL)]
    partners += [to_yup, to_ydown, to_hup, to_hdown, sibling]
    for partner in partners:
        pl.semaphore_signal(barrier, inc=1, device_id=partner, device_id_type=pl.DeviceIdType.MESH)
    pl.semaphore_wait(barrier, len(partners))

    w_z = [send(wz.at[zl], wz.at[zl], at(zl=(zl + d) % NL)) for d in range(1, NL)]
    load_c.wait()
    c_up = send(cot.at[tn], cot.at[tn], to_hup)
    c_down = send(cot.at[tn], cot.at[tn], to_hdown)
    c_sib = [send(cot.at[tn], cot.at[tn], sibling)]
    for copy in w_z:
        copy.wait_recv()

    wa[1, x] = wz[:, 0]
    wa_x = [send(wz.at[:, 0], wa.at[1, x], at(x=(x + d) % NX)) for d in range(1, NX)]

    def wa_step(k, before):
        new = []
        for q in range(2):
            for side, place, there, where in ((0, 1 - k, -k, to_yup), (1, 1 + k, 2 + k, to_ydown)):
                if k == 3 and q != side:
                    continue
                if before:
                    before[2 * q + side].wait_recv()
                xs = pl.ds(2 * q, 2)
                new.append(send(wa.at[place % NY, xs], wa.at[there % NY, xs], where))
        return new

    def wb_step(k, before):
        new = []
        for side, place, there, where in ((0, 1 - k, -k, to_yup), (1, 1 + k, 2 + k, to_ydown)):
            if before:
                before[side].wait_recv()
            src, dst = (wb.at[x, i % NY] for i in (place, there))
            if k == 3:
                lanes = pl.ds(128 * side, 128)
                src, dst = src.at[:, :, lanes], dst.at[:, :, lanes]
            new.append(send(src, dst, where))
        return new

    def wb_along_x(n):
        block = wb.at[x, pl.ds(4 * n, 4)]
        return send(block, block, to_xup), send(block, block, to_xdown)

    def wait(copies):
        for copy in copies:
            copy.wait_recv()

    wb[x, 1] = wz[:, 1]
    b_ring = wb_step(0, None)
    b_ring = wb_step(1, b_ring)
    wait(wa_x)
    a_ring = wa_step(0, None)
    wait(b_ring)
    b_x0 = wb_along_x(0)
    b_ring = wb_step(2, None)
    b_ring = wb_step(3, b_ring)
    a_ring = wa_step(1, a_ring)
    b_x0[0].wait_recv()
    block = wb.at[x_down, pl.ds(0, 4)]
    b_far0 = send(block, block, to_xup)
    wait(b_ring)
    b_x1 = wb_along_x(1)
    a_ring = wa_step(2, a_ring)

    lo, hi = pl.ds(0, 64), pl.ds(64, 64)
    c_up.wait_recv()
    from_down = cot.at[h_down * 2 + core]
    c_far0 = send(from_down.at[lo], from_down.at[lo], to_hup)
    c_down.wait_recv()
    from_up = cot.at[h_up * 2 + core]
    c_far1 = send(from_up.at[hi], from_up.at[hi], to_hdown)
    c_sib.append(send(from_down, from_down, sibling))
    c_sib.append(send(from_up, from_up, sibling))

    b_x1[1].wait_recv()
    block = wb.at[x_up, pl.ds(4, 4)]
    b_far1 = send(block, block, to_xdown)
    a_last = wa_step(3, a_ring)
    wait((a_ring[1], a_ring[2]))

    def assemble(n):
        for place in range(4 * n, 4 * n + 4):
            for run in range(NL):
                for half, src in ((0, wa[place, :, run]), (1, wb[:, place, run])):
                    wide = src.astype(F32)
                    for quarter in range(2):
                        rows = wide[:, 8 * quarter : 8 * quarter + 8].reshape(32, 256).astype(BF16)
                        at_lane = 512 * half + 256 * quarter
                        wall[place * NL + run, :, at_lane : at_lane + 256] = rows

    def key_product(n):
        out = []
        for j, h in enumerate((h_far, h_up, h_down, zh)):
            rows = pl.ds(pl.multiple_of(h * 256, 256), 256)
            prod = lax.dot_general(
                x_v[rows, :], wall[12 * n : 12 * n + 12].reshape(384, 1024), (((1,), (1,)), ((), ())),
                preferred_element_type=F32,
            )
            part[n, j] = prod.reshape(2, 128, 384)
            out.append(send(part.at[n, j, 1 - core], part_in.at[n, j], sibling))
        return out

    def key_first(n, halves):
        def join(j):
            halves[j].wait_recv()
            part[n, j, core] = part[n, j, core] + part_in[n, j]

        join(0)
        a0 = send(part.at[n, 0, core, lo], key_a.at[n, 0], to_hup)
        a1 = send(part.at[n, 0, core, hi], key_a.at[n, 1], to_hdown)
        join(1)
        join(2)
        join(3)
        return a0, a1, []

    def key_own(n, flows):
        flows[2].append(send(part.at[n, 1, core, hi], key_b.at[n, 0, hi], to_hup))
        flows[2].append(send(part.at[n, 2, core, lo], key_b.at[n, 1, lo], to_hdown))

    def key_relay(n, flows):
        a0, a1, b = flows
        a0.wait_recv()
        part[n, 1, core, lo] = part[n, 1, core, lo] + key_a[n, 0]
        b.append(send(part.at[n, 1, core, lo], key_b.at[n, 0, lo], to_hup))
        a1.wait_recv()
        part[n, 2, core, hi] = part[n, 2, core, hi] + key_a[n, 1]
        b.append(send(part.at[n, 2, core, hi], key_b.at[n, 1, hi], to_hdown))
        return b

    load_x.wait()
    wait((b_x0[1], b_far0))
    assemble(0)
    halves0 = key_product(0)
    wait((b_x1[0], b_far1))
    wait(a_last)
    flows0 = key_first(0, halves0)
    assemble(1)
    halves = key_product(1)

    c_far0.wait_recv()
    c_far1.wait_recv()
    far = cot.at[h_far * 2 + core]
    c_sib.append(send(far, far, sibling))
    flows1 = key_first(1, halves)
    key_own(0, flows0)
    for copy in c_sib:
        copy.wait_recv()

    for q in range(3):
        left = cot[:, :, 256 * q : 256 * q + 256].reshape(1024, 256)
        prod = lax.dot_general(left, x_v[...], (((0,), (0,)), ((), ())), preferred_element_type=F32)
        g[8 * q : 8 * q + 8] = prod.reshape(8, 32, 1024)

    fa, fb = pl.ds(0, 512), pl.ds(512, 512)
    size = NL // SUBS_G

    def a_first(q):
        far_y = ((y + 4) % NY) * NL + q * size
        at_q = pl.ds(q * size, size)
        a = send(g.at[pl.ds(far_y, size), pl.ds(0, 16), fa], a_half.at[0, at_q], to_yup)
        b = send(g.at[pl.ds(far_y, size), pl.ds(16, 16), fa], a_half.at[1, at_q], to_ydown)
        return a, b

    def a_step(k, q, before):
        at_q = pl.ds(q * size, size)
        up = ((y + 4 - k) % NY) * NL + q * size
        down = ((y + 4 + k) % NY) * NL + q * size
        new = []
        for side, block, where in ((0, up, to_yup), (1, down, to_ydown)):
            before[side].wait_recv()
            here = pl.ds(block, size)
            if k == 1:
                rows = pl.ds(16 * side, 16)
                g[here, rows, fa] = g[here, rows, fa] + a_half[side, at_q]
            else:
                g[here, :, fa] = g[here, :, fa] + a_in[side, k - 2, at_q]
            new.append(send(g.at[here, :, fa], a_in.at[side, k - 1, at_q], where))
        return new

    first, last = pl.ds(0, 12), pl.ds(12, 12)

    def rows_of(to):
        return pl.ds(pl.multiple_of(to * 8, 8), 8)

    a_flow = [a_first(q) for q in range(SUBS_G)]
    g_far0 = send(g.at[first, rows_of(x_far), fb], bx_a.at[0], to_xup)
    g_far1 = send(g.at[last, rows_of(x_far), fb], bx_a.at[1], to_xdown)
    g_x = [
        send(g.at[last, rows_of(x_up), fb], bx_in.at[0, last], to_xup),
        send(g.at[first, rows_of(x_down), fb], bx_in.at[1, first], to_xdown),
    ]

    for place in range(NY):
        wabs[pl.ds(((y + NY - 1 + place) % NY) * NL, NL)] = wall[NL * place : NL * place + NL]

    def grad_chunk(i):
        prod = jnp.dot(
            cot[2 * i : 2 * i + 2].reshape(256, 768), wabs[...].reshape(768, 1024), preferred_element_type=F32
        )
        grad_v[256 * i : 256 * i + 256] = prod.astype(BF16)

    grad_chunk(0)
    grad_chunk(1)
    for q in range(SUBS_G):
        a_flow[q] = a_step(1, q, a_flow[q])
    g_far0.wait_recv()
    g[first, rows_of(x_up), fb] = g[first, rows_of(x_up), fb] + bx_a[0]
    g_x.append(send(g.at[first, rows_of(x_up), fb], bx_in.at[0, first], to_xup))
    g_far1.wait_recv()
    g[last, rows_of(x_down), fb] = g[last, rows_of(x_down), fb] + bx_a[1]
    g_x.append(send(g.at[last, rows_of(x_down), fb], bx_in.at[1, last], to_xdown))
    k_b0 = key_relay(0, flows0)
    key_own(1, flows1)
    grad_chunk(2)
    grad_chunk(3)
    store_grad = pltpu.make_async_copy(grad_v, grad_hbm, local_sems.at[2])
    store_grad.start()
    for q in range(SUBS_G):
        a_flow[q] = a_step(2, q, a_flow[q])

    for copy in g_x:
        copy.wait_recv()
    b_sum[...] = g[:, rows_of(x), fb] + (bx_in[0] + bx_in[1])

    def b_step(k, before):
        new = []
        for side, place, where in ((0, y + 4 - k, to_yup), (1, y + 4 + k, to_ydown)):
            here = pl.ds((place % NY) * NL, NL)
            lanes = pl.ds(256 * side, 256)
            if k > 0:
                before[side].wait_recv()
            if k == 0:
                new.append(send(b_sum.at[here, :, lanes], b_half.at[side], where))
                continue
            if k == 1:
                b_sum[here, :, lanes] = b_sum[here, :, lanes] + b_half[side]
            else:
                b_sum[here] = b_sum[here] + b_in[side, k - 2]
            new.append(send(b_sum.at[here], b_in.at[side, k - 1], where))
        return new

    b_flow = b_step(0, None)
    for q in range(SUBS_G):
        a_flow[q] = a_step(3, q, a_flow[q])
    b_flow = b_step(1, b_flow)
    k_b1 = key_relay(1, flows1)
    b_flow = b_step(2, b_flow)
    b_flow = b_step(3, b_flow)
    for q in range(SUBS_G):
        a_flow[q][0].wait_recv()
        a_flow[q][1].wait_recv()
    own = pl.ds(y * NL, NL)
    g[own, :, fa] = g[own, :, fa] + (a_in[0, 2] + a_in[1, 2])
    a_x = []
    for d in range(1, NX):
        to = (x + d) % NX
        a_x.append(send(g.at[own, rows_of(to), fa], ax_in.at[x], at(x=to)))
    ax_in[x] = g[own, rows_of(x), fa]
    for copy in b_flow:
        copy.wait_recv()
    gz[pl.ds(3, 3), :, fb] = b_sum[own] + (b_in[0, 2] + b_in[1, 2])
    for copy in a_x:
        copy.wait_recv()
    gz[pl.ds(3, 3), :, fa] = (ax_in[0] + ax_in[1]) + (ax_in[2] + ax_in[3])

    g_z = []
    for d in range(1, NL):
        to = (zl + d) % NL
        g_z.append(send(gz.at[3 + to], gz.at[d], at(zl=to)))

    turn = ((y + NY - 1) % NY) * 96
    gap = lax.broadcasted_iota(jnp.int32, (768, 768), 1) - lax.broadcasted_iota(jnp.int32, (768, 768), 0)
    back = jnp.where((gap == turn) | (gap == turn - 768), 1.0, 0.0).astype(BF16)
    keys = None
    for n, copies in ((0, k_b0), (1, k_b1)):
        for copy in copies:
            copy.wait_recv()
        rel = (part[n, 3, core] + (key_b[n, 0] + key_b[n, 1])).astype(BF16)
        term = jnp.dot(rel, back[384 * n : 384 * n + 384], preferred_element_type=F32)
        keys = term if keys is None else keys + term
    key_ref[...] = keys.astype(BF16)

    for copy in g_z:
        copy.wait_recv()
    wg_ref[...] = gz[3 + zl] + gz[1] + gz[2]

    for copy in sends:
        copy.wait_send()
    store_grad.wait()


def body(inputs, key_weight, key_cotangent):
    vmem = pl.BlockSpec(memory_space=pltpu.VMEM)
    hbm = pl.BlockSpec(memory_space=pl.ANY)
    return pl.pallas_call(
        kernel,
        out_shape=(
            jax.ShapeDtypeStruct((128, 768), BF16),
            jax.ShapeDtypeStruct((1024, 1024), BF16),
            jax.ShapeDtypeStruct((8, 1024), F32),
        ),
        in_specs=[hbm, vmem, hbm],
        out_specs=(vmem, hbm, vmem),
        scratch_shapes=[
            pltpu.VMEM((1024, 1024), BF16),
            pltpu.VMEM((NL, 2, 16, 256), BF16),
            pltpu.VMEM((NY, NX, NL, 16, 256), BF16),
            pltpu.VMEM((NX, NY, NL, 16, 256), BF16),
            pltpu.VMEM((24, 32, 1024), BF16),
            pltpu.VMEM((24, 32, 1024), BF16),
            pltpu.VMEM((8, 128, 768), BF16),
            pltpu.VMEM((2, 4, 2, 128, 384), F32),
            pltpu.VMEM((2, 4, 128, 384), F32),
            pltpu.VMEM((2, 2, 64, 384), F32),
            pltpu.VMEM((2, 2, 128, 384), F32),
            pltpu.VMEM((24, 32, 1024), F32),
            pltpu.VMEM((2, 3, 16, 512), F32),
            pltpu.VMEM((2, 3, 3, 32, 512), F32),
            pltpu.VMEM((NX, NL, 8, 512), F32),
            pltpu.VMEM((2, 12, 8, 512), F32),
            pltpu.VMEM((2, 24, 8, 512), F32),
            pltpu.VMEM((24, 8, 512), F32),
            pltpu.VMEM((2, 3, 8, 256), F32),
            pltpu.VMEM((2, 3, 3, 8, 512), F32),
            pltpu.VMEM((6, 8, 1024), F32),
            pltpu.VMEM((1024, 1024), BF16),
            pltpu.SemaphoreType.DMA((N_COPIES,)),
            pltpu.SemaphoreType.DMA((N_COPIES,)),
            pltpu.SemaphoreType.DMA((3,)),
        ],
        compiler_params=pltpu.CompilerParams(
            collective_id=0, has_side_effects=True, vmem_limit_bytes=VMEM_MIB * 1024 * 1024
        ),
        cost_estimate=pl.CostEstimate(flops=4_831_838_208, bytes_accessed=5_000_000, transcendentals=0),
    )(inputs, key_weight, key_cotangent)


def solution(mesh):
    in_specs = (P("dp", "tensor"), P("dp", "tensor"), P(("dp", "tensor"), None))
    out_specs = (P(("dp", "tensor"), None), P("dp", "tensor"), P("dp", "tensor"))
    return jax.shard_map(body, mesh=mesh, in_specs=in_specs, out_specs=out_specs, check_vma=False)
```
